32 devices in a mesh: leaf: 8 (over z, y), front: 4 (over x, core).
Axes of the slice: x: 2, y: 2, z: 4, core: 2. Of those that a mesh axis runs over, the one named last changes fastest.
Arguments:
- right_side: bfloat16 [32, 40960], P(None, ('leaf', 'front')), may hold values from -6 to 6
- send_order: int32 [40960], P(('leaf', 'front')), may hold values from 0 to 1279, as said below
- owner_order: int32 [40960], P(('leaf', 'front')), may hold values from 0 to 1279, as said below
- live_rows: int32 [7], replicated, may hold values from 2048 to 4096, as said below
- lower_leaf: bfloat16 [1536, 12288], P(None, ('leaf', 'front')), may hold values from -0.109375 to 0.109375
- upper_leaf: bfloat16 [1536, 12288], P(None, ('leaf', 'front')), may hold values from -0.109375 to 0.109375
- lower_first: bfloat16 [4096, 16384], P(None, ('leaf', 'front')), may hold values from -0.0625 to 0.0625
- lower_second: bfloat16 [4096, 8192], P(None, ('leaf', 'front')), may hold values from -0.0625 to 0.0625
- lower_third: bfloat16 [4096, 4096], P(None, ('leaf', 'front')), may hold values from -0.0625 to 0.0625
- upper_first: bfloat16 [4096, 16384], P(None, ('leaf', 'front')), may hold values from -0.0625 to 0.0625
- upper_second: bfloat16 [4096, 8192], P(None, ('leaf', 'front')), may hold values from -0.0625 to 0.0625
- upper_third: bfloat16 [4096, 4096], P(None, ('leaf', 'front')), may hold values from -0.0625 to 0.0625
- downlink_first: bfloat16 [4096, 12288], P(None, ('leaf', 'front')), may hold values from -0.21875 to 0.21875
- downlink_second: bfloat16 [4096, 16384], P(None, ('leaf', 'front')), may hold values from -0.125 to 0.125
- downlink_third: bfloat16 [4096, 8192], P(None, ('leaf', 'front')), may hold values from -0.125 to 0.125
- uplink_first: bfloat16 [4096, 12288], P(None, ('leaf', 'front')), may hold values from -0.0625 to 0.0625
- uplink_second: bfloat16 [4096, 16384], P(None, ('leaf', 'front')), may hold values from -0.0625 to 0.0625
- uplink_third: bfloat16 [4096, 8192], P(None, ('leaf', 'front')), may hold values from -0.0625 to 0.0625
- pattern_first: int32 [64, 192], P(None, ('leaf', 'front')), may hold values 0 or 1
- pattern_second: int32 [64, 256], P(None, ('leaf', 'front')), may hold values 0 or 1
- pattern_third: int32 [64, 128], P(None, ('leaf', 'front')), may hold values 0 or 1
Outputs:
- solution: bfloat16 [32, 40960], P(None, ('leaf', 'front'))
The draws below stay inside these ranges and needn't reach their ends.
Inputs may be any that keep to these rules, and one draw needn't show every extreme that they name: `send_order`: each device's 1280 entries are a permutation of 0 to 1279. `owner_order`: each device's 1280 entries are a permutation of 0 to 1279. `live_rows`: multiples of 64.
All inputs are finite; a program needn't handle non-finite values. No bound on the sum of `pattern_first` or of `pattern_second` or of `pattern_third` on one device may be relied on, other than what follows from the above.
Results may differ from the reference program's by a relative error of at most 0.023.
Values may be sent and summed in bfloat16 or wider, within the bound.
A program may use at most 128 MiB of HBM per device.

```python
import jax
import jax.numpy as jnp

KRYLOV = 32
SEP = 4096
LEAF_FRONT = 1536
BLOCK = 64
ROWS_DEV = 1280
ROWS = 40960
NODES = 7
N_LEAF = 8
N_FRONT = 4


def device_orders(key):
    keys = jax.random.split(key, ROWS // ROWS_DEV)
    orders = jax.vmap(lambda single: jax.random.permutation(single, ROWS_DEV))(keys)
    return orders.reshape(-1).astype(jnp.int32)


def draw_send_order(key, part):
    return device_orders(jax.random.fold_in(key, 11))


def draw_owner_order(key, part):
    return device_orders(jax.random.fold_in(key, 23))


def draw_live_rows(key, part):
    first_key = jax.random.fold_in(key, 37)
    second_key = jax.random.fold_in(key, 41)
    counts = jax.random.randint(first_key, (NODES,), SEP // (2 * BLOCK), SEP // BLOCK + 1)
    chosen = jax.random.randint(second_key, (), 0, NODES)
    values = jnp.where(jnp.arange(NODES) == chosen, SEP // BLOCK, counts) * BLOCK
    return values.astype(jnp.int32)


def touch_ends(array, key, least, high):
    longest = array.shape.index(max(array.shape))
    spots = []
    for shift in (0, 1):
        where = [jax.random.randint(jax.random.fold_in(key, axis), (), 0, length) for axis, length in enumerate(array.shape)]
        where[longest] = (where[longest] + shift) % array.shape[longest]
        spots.append(tuple(where))
    return array.at[spots[0]].set(least).at[spots[1]].set(high)


def raised(values, stream_key, source, target, shards_of, factor):
    def block_of(position):
        return (jnp.arange(values.shape[position]) // (values.shape[position] // shards_of)).reshape((-1,) + (1,) * (values.ndim - 1 - position))

    one_side = jax.random.permutation(stream_key, shards_of)[block_of(target)]
    second = (block_of(target) + shards_of // 2) % shards_of
    return jnp.where((block_of(source) == one_side) | (block_of(source) == second), factor * values, values)


def steps_of(rng, extent, cuts, smallest, high):
    loudness, own = 1.0, jax.random.fold_in(rng, 6)
    for position, parts in cuts:
        heights = jnp.exp(jax.random.uniform(jax.random.fold_in(own, position), (parts,), jnp.float32, smallest / len(cuts), high / len(cuts)))
        loudness = loudness * jnp.repeat(heights, extent[position] // parts).reshape([-1 if axis == position else 1 for axis in range(len(extent))])
    return loudness


def normal_values(key, shape, scale, reach, cuts=(), held_as=jnp.bfloat16):
    drawn = jax.random.normal(key, shape, jnp.float32) * scale
    if len(cuts) > 0:
        drawn = steps_of(key, shape, cuts, -0.22, 0.18) * drawn
    return jnp.clip(drawn, min=-reach, max=reach).astype(held_as)


def bell_draw_with(key, shape, width, bound, shards, heavy, held_as=jnp.bfloat16):
    array = width * jax.random.normal(key, shape, jnp.float32)
    if shards:
        array = array * steps_of(key, shape, shards, -0.22, 0.18)
    return jnp.clip(raised(array, jax.random.fold_in(key, 3), *heavy), -bound, bound).astype(held_as)


def setup_inputs(seed: int = 0) -> dict:
    key_of = jax.random.split(jax.random.key(seed), 22)
    return {
        "right_side": normal_values(key_of[0], (KRYLOV, ROWS), 1.0, 6.0, ((1, 32),)),
        "send_order": draw_send_order(jax.random.fold_in(key_of[21], 71), 0),
        "owner_order": draw_owner_order(jax.random.fold_in(key_of[21], 71), 0),
        "live_rows": draw_live_rows(jax.random.fold_in(key_of[21], 71), 0),
        "lower_leaf": normal_values(key_of[4], (LEAF_FRONT, N_LEAF * LEAF_FRONT), (2 * LEAF_FRONT) ** -0.5, 0.109375, ((1, 32),)),
        "upper_leaf": normal_values(key_of[5], (LEAF_FRONT, N_LEAF * LEAF_FRONT), (2 * LEAF_FRONT) ** -0.5, 0.109375, ((1, 32),)),
        "lower_first": normal_values(key_of[6], (SEP, N_LEAF // 2 * SEP), (2 * SEP) ** -0.5, 0.0625, ((1, 32),)),
        "lower_second": normal_values(key_of[7], (SEP, N_LEAF // 4 * SEP), (2 * SEP) ** -0.5, 0.0625, ((1, 32),)),
        "lower_third": normal_values(key_of[8], (SEP, N_LEAF // 8 * SEP), (2 * SEP) ** -0.5, 0.0625, ((1, 32),)),
        "upper_first": normal_values(key_of[9], (SEP, N_LEAF // 2 * SEP), (2 * SEP) ** -0.5, 0.0625, ((1, 32),)),
        "upper_second": normal_values(key_of[10], (SEP, N_LEAF // 4 * SEP), (2 * SEP) ** -0.5, 0.0625, ((1, 32),)),
        "upper_third": normal_values(key_of[11], (SEP, N_LEAF // 8 * SEP), (2 * SEP) ** -0.5, 0.0625, ((1, 32),)),
        "downlink_first": bell_draw_with(key_of[12], (SEP, N_LEAF * LEAF_FRONT), (2 * LEAF_FRONT) ** -0.5, 0.21875, ((1, 32),), (1, 0, 32, 2.75)),
        "downlink_second": bell_draw_with(key_of[13], (SEP, N_LEAF // 2 * SEP), (2 * SEP) ** -0.5, 0.125, ((1, 32),), (1, 0, 32, 2.75)),
        "downlink_third": bell_draw_with(key_of[14], (SEP, N_LEAF // 4 * SEP), (2 * SEP) ** -0.5, 0.125, ((1, 32),), (1, 0, 32, 2.75)),
        "uplink_first": normal_values(key_of[15], (SEP, N_LEAF * LEAF_FRONT), (2 * SEP) ** -0.5, 0.0625, ((1, 32),)),
        "uplink_second": normal_values(key_of[16], (SEP, N_LEAF // 2 * SEP), (2 * SEP) ** -0.5, 0.0625, ((1, 32),)),
        "uplink_third": normal_values(key_of[17], (SEP, N_LEAF // 4 * SEP), (2 * SEP) ** -0.5, 0.0625, ((1, 32),)),
        "pattern_first": touch_ends((jax.random.randint(key_of[18], (SEP // BLOCK, N_LEAF * LEAF_FRONT // BLOCK), 0, 4) < 3).astype(jnp.int32), jax.random.fold_in(key_of[18], 1), 0, 1),
        "pattern_second": touch_ends((jax.random.randint(key_of[19], (SEP // BLOCK, N_LEAF // 2 * SEP // BLOCK), 0, 4) < 3).astype(jnp.int32), jax.random.fold_in(key_of[19], 1), 0, 1),
        "pattern_third": touch_ends((jax.random.randint(key_of[20], (SEP // BLOCK, N_LEAF // 4 * SEP // BLOCK), 0, 4) < 3).astype(jnp.int32), jax.random.fold_in(key_of[20], 1), 0, 1),
    }


def spread(pattern, block):
    wide = jnp.repeat(pattern, block, axis=0)
    return jnp.repeat(wide, block, axis=1).astype(jnp.bfloat16)


def reference(right_side, send_order, owner_order, live_rows, lower_leaf, upper_leaf, lower_first, lower_second, lower_third, upper_first, upper_second, upper_third, downlink_first, downlink_second, downlink_third, uplink_first, uplink_second, uplink_third, pattern_first, pattern_second, pattern_third):
    devices = N_LEAF * N_FRONT
    pair_rows = ROWS_DEV // devices
    sender = send_order.reshape(devices, ROWS_DEV)
    owner = owner_order.reshape(devices, ROWS_DEV)
    source = owner // pair_rows
    slot_in = owner % pair_rows
    target = jnp.arange(devices, dtype=jnp.int32)[:, None]
    local = sender[source, target * pair_rows + slot_in]
    anchor = (source * ROWS_DEV + local).reshape(-1).astype(jnp.int32)
    front = jnp.take(right_side, anchor, axis=1).reshape(KRYLOV, N_LEAF, N_FRONT, ROWS_DEV)
    leaf_dev = LEAF_FRONT // N_FRONT
    leaf_rhs = front[:, :, :, :leaf_dev].reshape(KRYLOV, N_LEAF, LEAF_FRONT)
    lowers = [lower_first, lower_second, lower_third]
    uppers = [upper_first, upper_second, upper_third]
    downs = [downlink_first, downlink_second, downlink_third]
    backs = [uplink_first, uplink_second, uplink_third]
    patterns = [pattern_first, pattern_second, pattern_third]
    starts = [0, N_LEAF // 2, N_LEAF // 2 + N_LEAF // 4]
    level_rhs = []
    masks = []
    offset = leaf_dev
    for level in range(1, 4):
        piece = SEP // (2 ** level * N_FRONT)
        nodes = N_LEAF // 2 ** level
        level_rhs.append(front[:, :, :, offset:offset + piece].reshape(KRYLOV, nodes, SEP))
        offset = offset + piece
        lives = live_rows[starts[level - 1]:starts[level - 1] + nodes]
        masks.append((jnp.arange(SEP, dtype=jnp.int32)[None, :] < lives[:, None]).astype(jnp.float32))
    leaf_y = []
    for group in range(N_LEAF):
        block_cols = lower_leaf[:, group * LEAF_FRONT:(group + 1) * LEAF_FRONT]
        leaf_y.append(jnp.dot(leaf_rhs[:, group], block_cols, preferred_element_type=jnp.float32).astype(jnp.bfloat16))
    children = leaf_y
    child_size = LEAF_FRONT
    level_y = []
    for level in range(1, 4):
        link = downs[level - 1] * spread(patterns[level - 1], BLOCK)
        found = []
        for node in range(N_LEAF // 2 ** level):
            total = level_rhs[level - 1][:, node].astype(jnp.float32)
            for child in (2 * node, 2 * node + 1):
                part_cols = link[:, child * child_size:(child + 1) * child_size]
                total = total - jnp.dot(children[child], part_cols.T, preferred_element_type=jnp.float32)
            mask_row = masks[level - 1][node][None, :]
            reduced = (total * mask_row).astype(jnp.bfloat16)
            solved = jnp.dot(reduced, lowers[level - 1][:, node * SEP:(node + 1) * SEP], preferred_element_type=jnp.float32)
            found.append((solved * mask_row).astype(jnp.bfloat16))
        level_y.append(found)
        children = found
        child_size = SEP
    level_x = [None, None, None]
    top = []
    for node in range(N_LEAF // 8):
        mask_row = masks[2][node][None, :]
        solved = jnp.dot(level_y[2][node], upper_third[:, node * SEP:(node + 1) * SEP], preferred_element_type=jnp.float32)
        top.append((solved * mask_row).astype(jnp.bfloat16))
    level_x[2] = top
    for level in (2, 1):
        back = backs[level] * spread(patterns[level], BLOCK)
        found = []
        for node in range(N_LEAF // 2 ** level):
            mask_row = masks[level - 1][node][None, :]
            parent = level_x[level][node // 2]
            update = level_y[level - 1][node].astype(jnp.float32) - jnp.dot(parent, back[:, node * SEP:(node + 1) * SEP], preferred_element_type=jnp.float32)
            reduced = (update * mask_row).astype(jnp.bfloat16)
            solved = jnp.dot(reduced, uppers[level - 1][:, node * SEP:(node + 1) * SEP], preferred_element_type=jnp.float32)
            found.append((solved * mask_row).astype(jnp.bfloat16))
        level_x[level - 1] = found
    back = uplink_first * spread(pattern_first, BLOCK)
    leaf_x = []
    for group in range(N_LEAF):
        parent = level_x[0][group // 2]
        update = leaf_y[group].astype(jnp.float32) - jnp.dot(parent, back[:, group * LEAF_FRONT:(group + 1) * LEAF_FRONT], preferred_element_type=jnp.float32)
        reduced = update.astype(jnp.bfloat16)
        leaf_x.append(jnp.dot(reduced, upper_leaf[:, group * LEAF_FRONT:(group + 1) * LEAF_FRONT], preferred_element_type=jnp.float32).astype(jnp.bfloat16))
    layout = [jnp.stack(leaf_x, axis=1).reshape(KRYLOV, N_LEAF, N_FRONT, leaf_dev)]
    for level in range(1, 4):
        piece = SEP // (2 ** level * N_FRONT)
        layout.append(jnp.stack(level_x[level - 1], axis=1).reshape(KRYLOV, N_LEAF, N_FRONT, piece))
    placed = jnp.concatenate(layout, axis=3).reshape(KRYLOV, ROWS)
    return jnp.zeros((KRYLOV, ROWS), jnp.bfloat16).at[:, anchor].set(placed)
```

```python
import functools

import jax
import jax.numpy as jnp
from jax import lax
from jax.experimental import pallas as pl
from jax.experimental.pallas import tpu as pltpu
from jax.sharding import PartitionSpec as P


def partner_2(value, axis, distance):
    mask = 2**distance
    pairs = [(source, source ^ mask) for source in range(lax.axis_size(axis))]
    return lax.ppermute(value, axis, pairs)


def spread(pattern, block):
    wide = jnp.repeat(pattern, block, axis=0)
    return jnp.repeat(wide, block, axis=1).astype(jnp.bfloat16)


def collect_group(portion, level, place):
    gathered = lax.all_gather(portion, "front", axis=1, tiled=True)
    for level_bit in range(level):
        partner = partner_2(gathered, "leaf", level_bit)
        upper_side = place >> level_bit & 1 == 1
        gathered = jnp.where(
            upper_side,
            jnp.concatenate([partner, gathered], axis=1),
            jnp.concatenate([gathered, partner], axis=1),
        )
    return gathered


def leaf_term(portion, matrix):
    return jnp.dot(portion, matrix, preferred_element_type=jnp.float32)


def per_device(
    right_side,
    send_order,
    owner_order,
    live_rows,
    lower_leaf,
    upper_leaf,
    lower_first,
    lower_second,
    lower_third,
    upper_first,
    upper_second,
    upper_third,
    downlink_first,
    downlink_second,
    downlink_third,
    uplink_first,
    uplink_second,
    uplink_third,
    pattern_first,
    pattern_second,
    pattern_third,
):
    fronts = lax.axis_size("front")
    leaves = lax.axis_size("leaf")
    place = lax.axis_index("leaf")
    column = lax.axis_index("front")
    columns = right_side.shape[0]
    leaf_rows = lower_leaf.shape[1]
    sep = lower_first.shape[0]
    lowers = [lower_first, lower_second, lower_third]
    uppers = [upper_first, upper_second, upper_third]
    downs = [downlink_first, downlink_second, downlink_third]
    backs = [uplink_first, uplink_second, uplink_third]
    patterns = [pattern_first, pattern_second, pattern_third]
    block = downlink_first.shape[0] // pattern_first.shape[0]
    pieces = [lower_first.shape[1], lower_second.shape[1], lower_third.shape[1]]
    starts = [0, leaves // 2, leaves // 2 + leaves // 4]
    outgoing = jnp.take(right_side, send_order, axis=1)
    arrived = lax.all_to_all(outgoing, ("leaf", "front"), split_axis=1, concat_axis=1, tiled=True)
    ordered = jnp.take(arrived, owner_order, axis=1)
    leaf_rhs = ordered[:, :leaf_rows]
    level_rhs = []
    offset = leaf_rows
    for level in range(1, 4):
        level_rhs.append(ordered[:, offset : offset + pieces[level - 1]])
        offset = offset + pieces[level - 1]
    piece_masks = []
    full_masks = []
    within = []
    for level in range(1, 4):
        group = 2**level
        member = place & group - 1
        node_live = lax.dynamic_index_in_dim(
            live_rows, starts[level - 1] + (place >> level), 0, keepdims=False
        )
        first_row = (member * fronts + column) * pieces[level - 1]
        piece_masks.append(
            (first_row + jnp.arange(pieces[level - 1], dtype=jnp.int32) < node_live).astype(
                jnp.float32
            )[None, :]
        )
        full_masks.append(
            (jnp.arange(sep, dtype=jnp.int32) < node_live).astype(jnp.float32)[None, :]
        )
        within.append(member)
    expanded = [spread(patterns[index], block) for index in range(3)]
    leaf_y = leaf_term(
        lax.all_gather(leaf_rhs, "front", axis=1, tiled=True), matrix=lower_leaf
    ).astype(jnp.bfloat16)
    children = leaf_y
    level_y = []
    for level in range(1, 4):
        group = 2**level
        piece = pieces[level - 1]
        member = within[level - 1]
        link = downs[level - 1] * expanded[level - 1]
        own_rhs = level_rhs[level - 1].astype(jnp.float32)
        shaped = link.reshape(group, fronts, piece, link.shape[1])
        term = jnp.einsum(
            "kc,jfpc->kfjp", children, shaped, preferred_element_type=jnp.float32
        ).reshape(columns, sep)
        first_row = (column * group + member) * piece
        current = lax.dynamic_slice_in_dim(term, first_row, piece, 1)
        term = lax.dynamic_update_slice_in_dim(term, current - own_rhs, first_row, 1)
        share = lax.psum_scatter(
            term.astype(jnp.bfloat16), "front", scatter_dimension=1, tiled=True
        ).astype(jnp.float32)
        for level_bit in reversed(range(level)):
            middle = share.shape[1] // 2
            lower_half = share[:, :middle]
            upper_half = share[:, middle:]
            high_side = place >> level_bit & 1 == 1
            keeping = jnp.where(high_side, upper_half, lower_half)
            sending = jnp.where(high_side, lower_half, upper_half)
            share = keeping + partner_2(sending.astype(jnp.bfloat16), "leaf", level_bit).astype(
                sending.dtype
            )
        reduced_piece = (-share * piece_masks[level - 1]).astype(jnp.bfloat16)
        reduced_full = collect_group(reduced_piece, level, place)
        solved = jnp.dot(reduced_full, lowers[level - 1], preferred_element_type=jnp.float32)
        found = (solved * piece_masks[level - 1]).astype(jnp.bfloat16)
        level_y.append(found)
        children = found
    level_x = [None, None, None]
    top_full = collect_group(level_y[2], 3, place)
    level_x[2] = (
        jnp.dot(top_full, upper_third, preferred_element_type=jnp.float32) * piece_masks[2]
    ).astype(jnp.bfloat16)
    for level in (2, 1):
        back = backs[level] * expanded[level]
        parent_full = collect_group(level_x[level], level + 1, place)
        update = level_y[level - 1].astype(jnp.float32) - jnp.dot(
            parent_full, back, preferred_element_type=jnp.float32
        )
        reduced = (update * piece_masks[level - 1]).astype(jnp.bfloat16)
        reduced_full = collect_group(reduced, level, place)
        solved = jnp.dot(reduced_full, uppers[level - 1], preferred_element_type=jnp.float32)
        level_x[level - 1] = (solved * piece_masks[level - 1]).astype(jnp.bfloat16)
    back = uplink_first * expanded[0]
    parent_full = collect_group(level_x[0], 1, place)
    update = (
        leaf_y.astype(jnp.float32) - jnp.dot(parent_full, back, preferred_element_type=jnp.float32)
    ).astype(jnp.bfloat16)
    leaf_x = leaf_term(
        lax.all_gather(update, "front", axis=1, tiled=True), matrix=upper_leaf
    ).astype(jnp.bfloat16)
    placed = jnp.concatenate([leaf_x, level_x[0], level_x[1], level_x[2]], axis=1)
    outbound = jnp.zeros_like(placed).at[:, owner_order].set(placed)
    returned = lax.all_to_all(outbound, ("leaf", "front"), split_axis=1, concat_axis=1, tiled=True)
    return jnp.zeros_like(returned).at[:, send_order].set(returned)


MESH = pl.DeviceIdType.MESH
LANE = 128
HALF = 64
CORES = 2
WEIGHTS = 14


class Place:
    def __init__(self, leaves, fronts):
        self.leaves = leaves
        self.fronts = fronts
        self.across = fronts // CORES
        self.leaf = lax.axis_index("leaf")
        front = lax.axis_index("front")
        self.front = front
        self.x = front // CORES
        self.core = front % CORES

    def chips(self, group):
        return group * self.across

    def me(self, group):
        return (self.leaf % group) * self.across + self.x

    def device(self, group, chip):
        base = self.leaf // group * group
        return (base + chip // self.across, (chip % self.across) * CORES + self.core)

    def sibling(self):
        return (self.leaf, self.x * CORES + 1 - self.core)


def drain(view, sem):
    pltpu.make_async_copy(view, view, sem).wait()


def chip_phase(place, group, source, slots, send_sem, recv_sem):
    count = place.chips(group)
    me = place.me(group)

    def step(r, carry):
        target = (me + count - r) % count
        pltpu.make_async_remote_copy(
            src_ref=source(target),
            dst_ref=slots.at[r],
            send_sem=send_sem,
            recv_sem=recv_sem,
            device_id=place.device(group, target),
            device_id_type=MESH,
        ).start()
        return carry

    lax.fori_loop(1, count, step, 0)


def chip_wait(count, slots, send_sem, recv_sem):
    view = slots.at[pl.ds(1, count - 1)]
    drain(view, recv_sem)
    drain(view, send_sem)


def core_copy(place, source, target, send_sem, recv_sem):
    copy = pltpu.make_async_remote_copy(
        src_ref=source,
        dst_ref=target,
        send_sem=send_sem,
        recv_sem=recv_sem,
        device_id=place.sibling(),
        device_id_type=MESH,
    )
    copy.start()
    return copy


def gather(place, group, value, slots, full, sems, beside=None):
    count = place.chips(group)
    me = place.me(group)
    mine = slots.at[place.core]
    width = value.shape[1]
    mine[0] = value
    chip_phase(place, group, lambda target: mine.at[0], mine, sems.at[0], sems.at[1])
    if beside is not None:
        beside()
    chip_wait(count, mine, sems.at[0], sems.at[1])
    copy = core_copy(place, mine, mine, sems.at[2], sems.at[3])
    copy.wait()
    for chip in range(count):
        slot = (chip + count - me) % count
        for core in range(CORES):
            start = (chip * CORES + core) * width
            full[:, start : start + width] = slots[core, slot]


def product(full, weight, depth):
    rows, cols = weight.shape
    chunk = 512 if depth % 1024 else 1024

    def step(index, total):
        at = pl.ds(pl.multiple_of(index * chunk, chunk), chunk)
        return total + jnp.dot(full[:, at], weight[at, :], preferred_element_type=jnp.float32)

    return lax.fori_loop(0, depth // chunk, step, jnp.zeros((full.shape[0], cols), jnp.float32))


def times_transposed(value, matrix):
    return lax.dot_general(
        value, matrix, (((1,), (1,)), ((), ())), preferred_element_type=jnp.float32
    )


def scatter_sum(place, group, value, link, terms, core_in, summed, chip_in, sems, beside=None):
    count = place.chips(group)
    me = place.me(group)
    width = terms.shape[3]
    chunk = 512
    each = chunk // width

    def step(index, carry):
        at = pl.ds(pl.multiple_of(index * chunk, chunk), chunk)
        part = times_transposed(value, link[at, :]).astype(jnp.bfloat16)
        for inner in range(each):
            piece = index * each + inner
            terms[piece % CORES, piece // CORES] = part[:, inner * width : (inner + 1) * width]
        return carry

    lax.fori_loop(0, link.shape[0] // chunk, step, 0)
    copy = core_copy(place, terms.at[1 - place.core], core_in, sems.at[0], sems.at[1])
    copy.wait()
    summed[...] = (
        terms[place.core].astype(jnp.float32) + core_in[...].astype(jnp.float32)
    ).astype(jnp.bfloat16)
    chip_phase(
        place, group, lambda target: summed.at[target], chip_in, sems.at[2], sems.at[3]
    )
    if beside is not None:
        beside()
    chip_wait(count, chip_in, sems.at[2], sems.at[3])
    total = summed[me].astype(jnp.float32)
    for slot in range(1, count):
        total = total + chip_in[slot].astype(jnp.float32)
    return total


def exchange(place, parts, core_in, merged, chip_in, full, sems, first=None, second=None):
    group = place.leaves
    count = place.chips(group)
    me = place.me(group)
    copy = core_copy(place, parts, core_in, sems.at[0], sems.at[1])
    if first is not None:
        first()
    copy.wait()
    lanes = lax.broadcasted_iota(jnp.int32, (parts.shape[1], LANE), 1) // HALF
    own = lanes == place.core

    def merge(chip, carry):
        other = pltpu.roll(core_in[chip].astype(jnp.float32), HALF, 1)
        merged[chip] = jnp.where(own, parts[chip].astype(jnp.float32), other).astype(jnp.bfloat16)
        return carry

    lax.fori_loop(0, count, merge, 0)
    chip_phase(
        place, group, lambda target: merged.at[target], chip_in, sems.at[2], sems.at[3]
    )
    chip_in[0] = merged[me]
    if second is not None:
        second()
    chip_wait(count, chip_in, sems.at[2], sems.at[3])
    for chip in range(count):
        full[:, chip * LANE : (chip + 1) * LANE] = chip_in[(chip + count - me) % count]


def one_hot(index, rows):
    spots = lax.broadcasted_iota(jnp.int32, (rows, index.shape[1]), 0)
    return jnp.where(spots == index, 1.0, 0.0).astype(jnp.bfloat16)


def solve_kernel(leaves, fronts, pieces, leaf_piece, *refs):
    rhs, send_at, own_at, live, pattern = refs[:5]
    sources = refs[5 : 5 + WEIGHTS]
    out = refs[5 + WEIGHTS]
    scratch = list(refs[6 + WEIGHTS :])

    def take(number):
        taken = scratch[:number]
        del scratch[:number]
        return taken

    weights = take(WEIGHTS)
    (weight_sem,) = take(1)
    send_hot, own_hot = take(2)
    ordered, full, wide = take(3)
    out_trip = take(5)
    back_trip = take(5)
    leaf_down, leaf_down_sem, leaf_up, leaf_up_sem = take(4)
    sums = [take(5) for _ in range(3)]
    gathers = [take(2) for _ in range(9)]

    place = Place(leaves, fronts)
    count = place.chips(leaves)
    me = place.me(leaves)
    barrier = pltpu.get_barrier_semaphore()

    def greet(r, carry):
        target = (me + count - r) % count
        pl.semaphore_signal(
            barrier, inc=1, device_id=place.device(leaves, target), device_id_type=MESH
        )
        return carry

    lax.fori_loop(1, count, greet, 0)
    pl.semaphore_signal(barrier, inc=1, device_id=place.sibling(), device_id_type=MESH)
    loads = [
        pltpu.make_async_copy(sources[i], weights[i], weight_sem.at[i]) for i in range(WEIGHTS)
    ]
    for load in loads:
        load.start()
    (lower_leaf, down_1, lower_1, down_2, lower_2, down_3, lower_3) = weights[:7]
    (upper_3, up_3, upper_2, up_2, upper_1, up_1, upper_leaf) = weights[7:]

    def masked(index, offset):
        def run():
            loads[index].wait()
            link = weights[index]
            columns = link.shape[1]
            block = link.shape[0] // pattern.shape[0]

            def step(row, carry):
                at = pl.ds(pl.multiple_of(row * block, block), block)
                kept = pattern[row][:, offset : offset + columns].astype(jnp.bfloat16)
                link[at, :] = link[at, :] * kept
                return carry

            lax.fori_loop(0, pattern.shape[0], step, 0)

        return run

    second_at = leaf_piece
    third_at = leaf_piece + pieces[0]
    starts = [0, leaves // 2, leaves // 2 + leaves // 4]
    masks = []
    for level in range(1, 4):
        group = 2**level
        piece = pieces[level - 1]
        rows_live = live[starts[level - 1] + place.leaf // group]
        first_row = ((place.leaf % group) * fronts + place.front) * piece
        spots = lax.broadcasted_iota(jnp.int32, (1, piece), 1) + first_row
        masks.append(jnp.where(spots < rows_live, 1.0, 0.0))

    tile = 2 * LANE
    parts, core_in, merged, chip_in, trip_sem = out_trip
    rows_dev = rhs.shape[1]

    def send_step(index, carry):
        hot = one_hot(send_at[index], rows_dev)
        send_hot[index] = hot
        moved = jnp.dot(rhs[...], hot, preferred_element_type=jnp.float32).astype(jnp.bfloat16)
        parts[2 * index] = moved[:, :LANE]
        parts[2 * index + 1] = moved[:, LANE:]
        return carry

    lax.fori_loop(0, send_hot.shape[0], send_step, 0)
    pl.semaphore_wait(barrier, count)

    def owner_fill():
        def step(index, carry):
            own_hot[index] = one_hot(own_at[index], own_hot.shape[1])
            return carry

        lax.fori_loop(0, own_hot.shape[0], step, 0)

    exchange(
        place, parts, core_in, merged, chip_in, wide, trip_sem,
        first=owner_fill, second=masked(1, 0),
    )
    for index in range(own_hot.shape[0]):
        ordered[:, index * tile : (index + 1) * tile] = jnp.dot(
            wide[...], own_hot[index], preferred_element_type=jnp.float32
        ).astype(jnp.bfloat16)

    gather(
        place, 1, ordered[:, :leaf_piece], leaf_down, full, leaf_down_sem,
        beside=masked(3, second_at),
    )
    loads[0].wait()
    leaf_depth = leaf_piece * fronts
    leaf_y = product(full, lower_leaf, leaf_depth).astype(jnp.bfloat16)

    sep = lower_1.shape[0]
    child = leaf_y
    level_y = []
    offset = leaf_piece
    chores = [masked(5, third_at), masked(8, third_at), masked(10, second_at)]
    late = [masked(12, 0), None, None]
    for level in range(1, 4):
        piece = pieces[level - 1]
        total = scatter_sum(
            place, 2**level, child, weights[2 * level - 1], *sums[level - 1],
            beside=chores[level - 1],
        )
        own = ordered[:, offset : offset + piece].astype(jnp.float32)
        offset = offset + piece
        reduced = ((own - total) * masks[level - 1]).astype(jnp.bfloat16)
        gather(place, 2**level, reduced, gathers[level - 1][0], full, gathers[level - 1][1],
               beside=late[level - 1])
        loads[2 * level].wait()
        solved = product(full, weights[2 * level], sep)
        child = (solved * masks[level - 1]).astype(jnp.bfloat16)
        level_y.append(child)

    gather(place, 8, level_y[2], gathers[3][0], full, gathers[3][1])
    loads[7].wait()
    found = (product(full, upper_3, sep) * masks[2]).astype(jnp.bfloat16)
    starts_at = [leaf_piece, leaf_piece + pieces[0], leaf_piece + pieces[0] + pieces[1]]
    ordered[:, starts_at[2] : starts_at[2] + pieces[2]] = found
    turn = 4
    for level, back, upper, load in ((2, up_3, upper_2, 9), (1, up_2, upper_1, 11)):
        gather(place, 2 ** (level + 1), found, gathers[turn][0], full, gathers[turn][1])
        update = level_y[level - 1].astype(jnp.float32) - product(full, back, sep)
        reduced = (update * masks[level - 1]).astype(jnp.bfloat16)
        gather(place, 2**level, reduced, gathers[turn + 1][0], full, gathers[turn + 1][1])
        turn = turn + 2
        loads[load].wait()
        found = (product(full, upper, sep) * masks[level - 1]).astype(jnp.bfloat16)
        ordered[:, starts_at[level - 1] : starts_at[level - 1] + pieces[level - 1]] = found
    gather(place, 2, found, gathers[8][0], full, gathers[8][1])
    update = (leaf_y.astype(jnp.float32) - product(full, up_1, sep)).astype(jnp.bfloat16)
    gather(place, 1, update, leaf_up, full, leaf_up_sem)
    loads[13].wait()
    ordered[:, :leaf_piece] = product(full, upper_leaf, leaf_depth).astype(jnp.bfloat16)

    parts, core_in, merged, chip_in, trip_sem = back_trip

    def return_step(index, carry):
        at = pl.ds(pl.multiple_of(index * tile, tile), tile)
        moved = jnp.zeros((rhs.shape[0], tile), jnp.float32)
        for inner in range(own_hot.shape[0]):
            moved = moved + times_transposed(
                ordered[:, inner * tile : (inner + 1) * tile], own_hot[inner, at, :]
            )
        moved = moved.astype(jnp.bfloat16)
        parts[2 * index] = moved[:, :LANE]
        parts[2 * index + 1] = moved[:, LANE:]
        return carry

    lax.fori_loop(0, count // 2, return_step, 0)
    exchange(place, parts, core_in, merged, chip_in, wide, trip_sem)

    for index in range(rows_dev // tile):
        moved = jnp.zeros((rhs.shape[0], tile), jnp.float32)
        for inner in range(send_hot.shape[0]):
            moved = moved + times_transposed(
                wide[:, inner * tile : (inner + 1) * tile],
                send_hot[inner, index * tile : (index + 1) * tile, :],
            )
        out[:, index * tile : (index + 1) * tile] = moved.astype(jnp.bfloat16)


def in_one_kernel(
    leaves,
    fronts,
    right_side,
    send_order,
    owner_order,
    live_rows,
    lower_leaf,
    upper_leaf,
    lower_first,
    lower_second,
    lower_third,
    upper_first,
    upper_second,
    upper_third,
    downlink_first,
    downlink_second,
    downlink_third,
    uplink_first,
    uplink_second,
    uplink_third,
    pattern_first,
    pattern_second,
    pattern_third,
):
    columns, rows_dev = right_side.shape
    devices = leaves * fronts
    share = rows_dev // devices
    chips = devices // CORES
    sep = lower_first.shape[0]
    block = sep // pattern_first.shape[0]
    leaf_piece = lower_leaf.shape[1]
    pieces = (lower_first.shape[1], lower_second.shape[1], lower_third.shape[1])
    tile = 2 * LANE
    send_at = jnp.pad(
        send_order.reshape(devices, share), ((0, 0), (0, HALF - share)), constant_values=-1
    ).reshape(-1, 1, tile)
    own_at = (owner_order // share * HALF + owner_order % share).reshape(-1, 1, tile)
    pattern = jnp.repeat(
        jnp.concatenate([pattern_first, pattern_second, pattern_third], axis=1), block, axis=1
    ).astype(jnp.float32)[:, None, :]
    weights = [
        lower_leaf, downlink_first, lower_first, downlink_second, lower_second, downlink_third,
        lower_third, upper_third, uplink_third, upper_second, uplink_second, upper_first,
        uplink_first, upper_leaf,
    ]
    half = jnp.bfloat16
    dma = pltpu.SemaphoreType.DMA
    scratch = [pltpu.VMEM(weight.shape, weight.dtype) for weight in weights]
    scratch += [dma((WEIGHTS,))]
    scratch += [
        pltpu.VMEM((chips // 2, rows_dev, tile), half),
        pltpu.VMEM((rows_dev // tile, chips * LANE, tile), half),
        pltpu.VMEM((columns, rows_dev), half),
        pltpu.VMEM((columns, sep), half),
        pltpu.VMEM((columns, chips * LANE), half),
    ]
    for _ in range(2):
        scratch += [pltpu.VMEM((chips, columns, LANE), half) for _ in range(4)] + [dma((4,))]
    across = fronts // CORES
    for _ in range(2):
        scratch += [pltpu.VMEM((CORES, across, columns, leaf_piece), half), dma((4,))]
    for level in range(1, 4):
        slots = (2**level * across, columns, pieces[level - 1])
        scratch += [pltpu.VMEM((CORES,) + slots, half)]
        scratch += [pltpu.VMEM(slots, half) for _ in range(3)] + [dma((4,))]
    for level in (1, 2, 3, 3, 3, 2, 2, 1, 1):
        slots = (CORES, 2**level * across, columns, pieces[level - 1])
        scratch += [pltpu.VMEM(slots, half), dma((4,))]
    vmem = pl.BlockSpec(memory_space=pltpu.VMEM)
    return pl.pallas_call(
        functools.partial(solve_kernel, leaves, fronts, pieces, leaf_piece),
        out_shape=jax.ShapeDtypeStruct((columns, rows_dev), half),
        in_specs=[vmem, vmem, vmem, pl.BlockSpec(memory_space=pltpu.SMEM), vmem]
        + [pl.BlockSpec(memory_space=pl.ANY)] * WEIGHTS,
        out_specs=vmem,
        scratch_shapes=scratch,
        compiler_params=pltpu.CompilerParams(
            collective_id=0, has_side_effects=True, vmem_limit_bytes=60 * 2**20
        ),
    )(right_side, send_at, own_at, live_rows, pattern, *weights)


def choose(leaves, fronts, right_side, send_order, owner_order, live_rows, *matrices):
    rows_dev = right_side.shape[1]
    widths = [matrices[index].shape[1] for index in (0, 2, 3, 4)]
    whole_lanes = all(width % LANE == 0 for width in widths)
    if whole_lanes and rows_dev % (2 * LANE) == 0 and rows_dev // (leaves * fronts) <= HALF:
        run = functools.partial(in_one_kernel, leaves, fronts)
    else:
        run = per_device
    return run(right_side, send_order, owner_order, live_rows, *matrices)


def solution(mesh):
    placed = (
        P(None, ("leaf", "front")),
        P(("leaf", "front")),
        P(("leaf", "front")),
        P(),
        P(None, ("leaf", "front")),
        P(None, ("leaf", "front")),
        P(None, ("leaf", "front")),
        P(None, ("leaf", "front")),
        P(None, ("leaf", "front")),
        P(None, ("leaf", "front")),
        P(None, ("leaf", "front")),
        P(None, ("leaf", "front")),
        P(None, ("leaf", "front")),
        P(None, ("leaf", "front")),
        P(None, ("leaf", "front")),
        P(None, ("leaf", "front")),
        P(None, ("leaf", "front")),
        P(None, ("leaf", "front")),
        P(None, ("leaf", "front")),
        P(None, ("leaf", "front")),
        P(None, ("leaf", "front")),
    )
    return jax.shard_map(
        functools.partial(choose, mesh.shape["leaf"], mesh.shape["front"]),
        mesh=mesh,
        in_specs=placed,
        out_specs=P(None, ("leaf", "front")),
        check_vma=False,
    )
```

```python
import functools

import jax
import jax.numpy as jnp
from jax import lax
from jax.experimental import pallas as pl
from jax.experimental.pallas import tpu as pltpu
from jax.sharding import PartitionSpec as P


def partner_2(value, axis, distance):
    mask = 2**distance
    pairs = [(source, source ^ mask) for source in range(lax.axis_size(axis))]
    return lax.ppermute(value, axis, pairs)


def spread(pattern, block):
    wide = jnp.repeat(pattern, block, axis=0)
    return jnp.repeat(wide, block, axis=1).astype(jnp.bfloat16)


def collect_group(portion, level, place):
    gathered = lax.all_gather(portion, "front", axis=1, tiled=True)
    for level_bit in range(level):
        partner = partner_2(gathered, "leaf", level_bit)
        upper_side = place >> level_bit & 1 == 1
        gathered = jnp.where(
            upper_side,
            jnp.concatenate([partner, gathered], axis=1),
            jnp.concatenate([gathered, partner], axis=1),
        )
    return gathered


def leaf_term(portion, matrix):
    return jnp.dot(portion, matrix, preferred_element_type=jnp.float32)


def per_device(
    right_side,
    send_order,
    owner_order,
    live_rows,
    lower_leaf,
    upper_leaf,
    lower_first,
    lower_second,
    lower_third,
    upper_first,
    upper_second,
    upper_third,
    downlink_first,
    downlink_second,
    downlink_third,
    uplink_first,
    uplink_second,
    uplink_third,
    pattern_first,
    pattern_second,
    pattern_third,
):
    fronts = lax.axis_size("front")
    leaves = lax.axis_size("leaf")
    place = lax.axis_index("leaf")
    column = lax.axis_index("front")
    columns = right_side.shape[0]
    leaf_rows = lower_leaf.shape[1]
    sep = lower_first.shape[0]
    lowers = [lower_first, lower_second, lower_third]
    uppers = [upper_first, upper_second, upper_third]
    downs = [downlink_first, downlink_second, downlink_third]
    backs = [uplink_first, uplink_second, uplink_third]
    patterns = [pattern_first, pattern_second, pattern_third]
    block = downlink_first.shape[0] // pattern_first.shape[0]
    pieces = [lower_first.shape[1], lower_second.shape[1], lower_third.shape[1]]
    starts = [0, leaves // 2, leaves // 2 + leaves // 4]
    outgoing = jnp.take(right_side, send_order, axis=1)
    arrived = lax.all_to_all(outgoing, ("leaf", "front"), split_axis=1, concat_axis=1, tiled=True)
    ordered = jnp.take(arrived, owner_order, axis=1)
    leaf_rhs = ordered[:, :leaf_rows]
    level_rhs = []
    offset = leaf_rows
    for level in range(1, 4):
        level_rhs.append(ordered[:, offset : offset + pieces[level - 1]])
        offset = offset + pieces[level - 1]
    piece_masks = []
    full_masks = []
    within = []
    for level in range(1, 4):
        group = 2**level
        member = place & group - 1
        node_live = lax.dynamic_index_in_dim(
            live_rows, starts[level - 1] + (place >> level), 0, keepdims=False
        )
        first_row = (member * fronts + column) * pieces[level - 1]
        piece_masks.append(
            (first_row + jnp.arange(pieces[level - 1], dtype=jnp.int32) < node_live).astype(
                jnp.float32
            )[None, :]
        )
        full_masks.append(
            (jnp.arange(sep, dtype=jnp.int32) < node_live).astype(jnp.float32)[None, :]
        )
        within.append(member)
    expanded = [spread(patterns[index], block) for index in range(3)]
    leaf_y = leaf_term(
        lax.all_gather(leaf_rhs, "front", axis=1, tiled=True), matrix=lower_leaf
    ).astype(jnp.bfloat16)
    children = leaf_y
    level_y = []
    for level in range(1, 4):
        group = 2**level
        piece = pieces[level - 1]
        member = within[level - 1]
        link = downs[level - 1] * expanded[level - 1]
        own_rhs = level_rhs[level - 1].astype(jnp.float32)
        shaped = link.reshape(group, fronts, piece, link.shape[1])
        term = jnp.einsum(
            "kc,jfpc->kfjp", children, shaped, preferred_element_type=jnp.float32
        ).reshape(columns, sep)
        first_row = (column * group + member) * piece
        current = lax.dynamic_slice_in_dim(term, first_row, piece, 1)
        term = lax.dynamic_update_slice_in_dim(term, current - own_rhs, first_row, 1)
        share = lax.psum_scatter(
            term.astype(jnp.bfloat16), "front", scatter_dimension=1, tiled=True
        ).astype(jnp.float32)
        for level_bit in reversed(range(level)):
            middle = share.shape[1] // 2
            lower_half = share[:, :middle]
            upper_half = share[:, middle:]
            high_side = place >> level_bit & 1 == 1
            keeping = jnp.where(high_side, upper_half, lower_half)
            sending = jnp.where(high_side, lower_half, upper_half)
            share = keeping + partner_2(sending.astype(jnp.bfloat16), "leaf", level_bit).astype(
                sending.dtype
            )
        reduced_piece = (-share * piece_masks[level - 1]).astype(jnp.bfloat16)
        reduced_full = collect_group(reduced_piece, level, place)
        solved = jnp.dot(reduced_full, lowers[level - 1], preferred_element_type=jnp.float32)
        found = (solved * piece_masks[level - 1]).astype(jnp.bfloat16)
        level_y.append(found)
        children = found
    level_x = [None, None, None]
    top_full = collect_group(level_y[2], 3, place)
    level_x[2] = (
        jnp.dot(top_full, upper_third, preferred_element_type=jnp.float32) * piece_masks[2]
    ).astype(jnp.bfloat16)
    for level in (2, 1):
        back = backs[level] * expanded[level]
        parent_full = collect_group(level_x[level], level + 1, place)
        update = level_y[level - 1].astype(jnp.float32) - jnp.dot(
            parent_full, back, preferred_element_type=jnp.float32
        )
        reduced = (update * piece_masks[level - 1]).astype(jnp.bfloat16)
        reduced_full = collect_group(reduced, level, place)
        solved = jnp.dot(reduced_full, uppers[level - 1], preferred_element_type=jnp.float32)
        level_x[level - 1] = (solved * piece_masks[level - 1]).astype(jnp.bfloat16)
    back = uplink_first * expanded[0]
    parent_full = collect_group(level_x[0], 1, place)
    update = (
        leaf_y.astype(jnp.float32) - jnp.dot(parent_full, back, preferred_element_type=jnp.float32)
    ).astype(jnp.bfloat16)
    leaf_x = leaf_term(
        lax.all_gather(update, "front", axis=1, tiled=True), matrix=upper_leaf
    ).astype(jnp.bfloat16)
    placed = jnp.concatenate([leaf_x, level_x[0], level_x[1], level_x[2]], axis=1)
    outbound = jnp.zeros_like(placed).at[:, owner_order].set(placed)
    returned = lax.all_to_all(outbound, ("leaf", "front"), split_axis=1, concat_axis=1, tiled=True)
    return jnp.zeros_like(returned).at[:, send_order].set(returned)


MESH = pl.DeviceIdType.MESH
LANE = 128
HALF = 64
CORES = 2
WEIGHTS = 14


class Place:
    def __init__(self, leaves, fronts):
        self.leaves = leaves
        self.fronts = fronts
        self.across = fronts // CORES
        self.leaf = lax.axis_index("leaf")
        front = lax.axis_index("front")
        self.front = front
        self.x = front // CORES
        self.core = front % CORES

    def chips(self, group):
        return group * self.across

    def me(self, group):
        return (self.leaf % group) * self.across + self.x

    def device(self, group, chip):
        base = self.leaf // group * group
        return (base + chip // self.across, (chip % self.across) * CORES + self.core)

    def sibling(self):
        return (self.leaf, self.x * CORES + 1 - self.core)


def drain(view, sem):
    pltpu.make_async_copy(view, view, sem).wait()


def chip_phase(place, group, source, slots, send_sem, recv_sem):
    count = place.chips(group)
    me = place.me(group)

    def step(r, carry):
        target = (me + count - r) % count
        pltpu.make_async_remote_copy(
            src_ref=source(target),
            dst_ref=slots.at[r],
            send_sem=send_sem,
            recv_sem=recv_sem,
            device_id=place.device(group, target),
            device_id_type=MESH,
        ).start()
        return carry

    lax.fori_loop(1, count, step, 0)


def chip_wait(count, slots, send_sem, recv_sem):
    view = slots.at[pl.ds(1, count - 1)]
    drain(view, recv_sem)
    drain(view, send_sem)


def core_copy(place, source, target, send_sem, recv_sem):
    copy = pltpu.make_async_remote_copy(
        src_ref=source,
        dst_ref=target,
        send_sem=send_sem,
        recv_sem=recv_sem,
        device_id=place.sibling(),
        device_id_type=MESH,
    )
    copy.start()
    return copy


def half_product(slots, weight, core, me):
    count = slots.shape[1]
    pieces = [slots[core, (chip + count - me) % count] for chip in range(count)]
    rows = weight[core]
    return jnp.dot(
        jnp.concatenate(pieces, axis=1),
        rows.reshape(count * rows.shape[1], rows.shape[2]),
        preferred_element_type=jnp.float32,
    )


def gather_product(place, group, value, slots, weight, sems, beside=None, load=None):
    count = place.chips(group)
    me = place.me(group)
    mine = slots.at[place.core]
    mine[0] = value
    chip_phase(place, group, lambda target: mine.at[0], mine, sems.at[0], sems.at[1])
    if beside is not None:
        beside()
    chip_wait(count, mine, sems.at[0], sems.at[1])
    copy = core_copy(place, mine, mine, sems.at[2], sems.at[3])
    if load is not None:
        load()
    total = half_product(slots, weight, place.core, me)
    copy.wait()
    return total + half_product(slots, weight, 1 - place.core, me)


def times_transposed(value, matrix):
    return lax.dot_general(
        value, matrix, (((1,), (1,)), ((), ())), preferred_element_type=jnp.float32
    )


def scatter_sum(place, group, value, link, terms, core_in, summed, chip_in, sems, beside=None):
    count = place.chips(group)
    me = place.me(group)
    width = terms.shape[3]
    each = 512 // width

    def half(core):
        for first in range(0, count, each):
            rows = link[core, first : first + each]
            part = times_transposed(value, rows.reshape(each * width, rows.shape[2]))
            part = part.astype(jnp.bfloat16)
            for inner in range(each):
                terms[core, first + inner] = part[:, inner * width : (inner + 1) * width]

    half(1 - place.core)
    copy = core_copy(place, terms.at[1 - place.core], core_in, sems.at[0], sems.at[1])
    half(place.core)
    copy.wait()
    summed[...] = (
        terms[place.core].astype(jnp.float32) + core_in[...].astype(jnp.float32)
    ).astype(jnp.bfloat16)
    chip_phase(
        place, group, lambda target: summed.at[target], chip_in, sems.at[2], sems.at[3]
    )
    if beside is not None:
        beside()
    chip_wait(count, chip_in, sems.at[2], sems.at[3])
    total = summed[me].astype(jnp.float32)
    for slot in range(1, count):
        total = total + chip_in[slot].astype(jnp.float32)
    return total


def exchange(place, parts, core_in, merged, chip_in, full, sems, first=None, second=None):
    group = place.leaves
    count = place.chips(group)
    me = place.me(group)
    copy = core_copy(place, parts, core_in, sems.at[0], sems.at[1])
    if first is not None:
        first()
    copy.wait()
    lanes = lax.broadcasted_iota(jnp.int32, (parts.shape[1], LANE), 1) // HALF
    own = lanes == place.core

    def merge(chip, carry):
        other = pltpu.roll(core_in[chip].astype(jnp.float32), HALF, 1)
        merged[chip] = jnp.where(own, parts[chip].astype(jnp.float32), other).astype(jnp.bfloat16)
        return carry

    lax.fori_loop(0, count, merge, 0)
    chip_phase(
        place, group, lambda target: merged.at[target], chip_in, sems.at[2], sems.at[3]
    )
    chip_in[0] = merged[me]
    if second is not None:
        second()
    chip_wait(count, chip_in, sems.at[2], sems.at[3])
    for chip in range(count):
        full[:, chip * LANE : (chip + 1) * LANE] = chip_in[(chip + count - me) % count]


def fill_hot(target, index):
    rows = 128

    def step(block, carry):
        first = pl.multiple_of(block * rows, rows)
        spots = lax.broadcasted_iota(jnp.int32, (rows, index.shape[1]), 0) + first
        target[pl.ds(first, rows), :] = jnp.where(spots == index, 1.0, 0.0).astype(jnp.bfloat16)
        return carry

    lax.fori_loop(0, target.shape[0] // rows, step, 0)


def solve_kernel(leaves, fronts, pieces, leaf_piece, *refs):
    rhs, send_at, own_at, live = refs[:4]
    patterns = refs[4:7]
    sources = refs[7 : 7 + WEIGHTS]
    out = refs[7 + WEIGHTS]
    scratch = list(refs[8 + WEIGHTS :])

    def take(number):
        taken = scratch[:number]
        del scratch[:number]
        return taken

    weights = take(WEIGHTS)
    (weight_sem,) = take(1)
    send_hot, own_hot = take(2)
    ordered, wide = take(2)
    out_trip = take(5)
    back_trip = take(5)
    leaf_down, leaf_down_sem, leaf_up, leaf_up_sem = take(4)
    sums = [take(5) for _ in range(3)]
    gathers = [take(2) for _ in range(9)]

    place = Place(leaves, fronts)
    count = place.chips(leaves)
    me = place.me(leaves)
    barrier = pltpu.get_barrier_semaphore()

    def greet(r, carry):
        target = (me + count - r) % count
        pl.semaphore_signal(
            barrier, inc=1, device_id=place.device(leaves, target), device_id_type=MESH
        )
        return carry

    lax.fori_loop(1, count, greet, 0)
    pl.semaphore_signal(barrier, inc=1, device_id=place.sibling(), device_id_type=MESH)
    loads = [
        [
            pltpu.make_async_copy(
                sources[i].at[:, core], weights[i].at[core], weight_sem.at[i, core]
            )
            for core in range(CORES)
        ]
        for i in range(WEIGHTS)
    ]
    for load in loads:
        for copy in load:
            copy.start()

    def ready(index):
        for copy in loads[index]:
            copy.wait()

    (lower_leaf, down_1, lower_1, down_2, lower_2, down_3, lower_3) = weights[:7]
    (upper_3, up_3, upper_2, up_2, upper_1, up_1, upper_leaf) = weights[7:]

    def masked(index, pattern):
        def run():
            ready(index)
            link = weights[index]
            width, columns = link.shape[2:]
            block = link.shape[1] * CORES * width // pattern.shape[0]
            each = width // block
            low = lax.broadcasted_iota(jnp.int32, (1, LANE), 1) < block

            def step(row, carry):
                kept = [
                    jnp.where(
                        low,
                        pattern[row, 2 * pair].astype(jnp.float32),
                        pattern[row, 2 * pair + 1].astype(jnp.float32),
                    )
                    for pair in range(columns // LANE)
                ]
                kept = jnp.concatenate(kept, axis=1).astype(jnp.bfloat16)
                piece = row // each
                at = pl.ds(pl.multiple_of(row % each * block, block), block)
                spot = (piece % CORES, piece // CORES, at)
                link[spot] = link[spot] * kept
                return carry

            lax.fori_loop(0, pattern.shape[0], step, 0)

        return run

    starts = [0, leaves // 2, leaves // 2 + leaves // 4]
    masks = []
    for level in range(1, 4):
        group = 2**level
        piece = pieces[level - 1]
        rows_live = live[starts[level - 1] + place.leaf // group]
        first_row = ((place.leaf % group) * fronts + place.front) * piece
        spots = lax.broadcasted_iota(jnp.int32, (1, piece), 1) + first_row
        masks.append(jnp.where(spots < rows_live, 1.0, 0.0))

    tile = 2 * LANE
    parts, core_in, merged, chip_in, trip_sem = out_trip
    rows_dev = rhs.shape[1]

    def send_step(index, carry):
        fill_hot(send_hot.at[index], send_at[index])
        moved = jnp.dot(rhs[...], send_hot[index], preferred_element_type=jnp.float32)
        moved = moved.astype(jnp.bfloat16)
        parts[2 * index] = moved[:, :LANE]
        parts[2 * index + 1] = moved[:, LANE:]
        return carry

    lax.fori_loop(0, send_hot.shape[0], send_step, 0)
    pl.semaphore_wait(barrier, count)

    def owner_fill():
        def step(index, carry):
            fill_hot(own_hot.at[index], own_at[index])
            return carry

        lax.fori_loop(0, own_hot.shape[0], step, 0)

    exchange(
        place, parts, core_in, merged, chip_in, wide, trip_sem,
        first=owner_fill, second=masked(1, patterns[0]),
    )
    for index in range(own_hot.shape[0]):
        ordered[:, index * tile : (index + 1) * tile] = jnp.dot(
            wide[...], own_hot[index], preferred_element_type=jnp.float32
        ).astype(jnp.bfloat16)

    leaf_y = gather_product(
        place, 1, ordered[:, :leaf_piece], leaf_down, lower_leaf, leaf_down_sem,
        beside=masked(3, patterns[1]), load=lambda: ready(0),
    ).astype(jnp.bfloat16)

    child = leaf_y
    level_y = []
    offset = leaf_piece
    chores = [masked(5, patterns[2]), masked(8, patterns[2]), masked(10, patterns[1])]
    late = [masked(12, patterns[0]), None, None]
    for level in range(1, 4):
        piece = pieces[level - 1]
        total = scatter_sum(
            place, 2**level, child, weights[2 * level - 1], *sums[level - 1],
            beside=chores[level - 1],
        )
        own = ordered[:, offset : offset + piece].astype(jnp.float32)
        offset = offset + piece
        reduced = ((own - total) * masks[level - 1]).astype(jnp.bfloat16)
        solved = gather_product(
            place, 2**level, reduced, gathers[level - 1][0], weights[2 * level],
            gathers[level - 1][1], beside=late[level - 1],
            load=functools.partial(ready, 2 * level),
        )
        child = (solved * masks[level - 1]).astype(jnp.bfloat16)
        level_y.append(child)

    found = gather_product(
        place, 8, level_y[2], gathers[3][0], upper_3, gathers[3][1],
        load=functools.partial(ready, 7),
    )
    found = (found * masks[2]).astype(jnp.bfloat16)
    starts_at = [leaf_piece, leaf_piece + pieces[0], leaf_piece + pieces[0] + pieces[1]]
    ordered[:, starts_at[2] : starts_at[2] + pieces[2]] = found
    turn = 4
    for level, back, upper, load in ((2, up_3, upper_2, 9), (1, up_2, upper_1, 11)):
        update = level_y[level - 1].astype(jnp.float32) - gather_product(
            place, 2 ** (level + 1), found, gathers[turn][0], back, gathers[turn][1]
        )
        reduced = (update * masks[level - 1]).astype(jnp.bfloat16)
        found = gather_product(
            place, 2**level, reduced, gathers[turn + 1][0], upper, gathers[turn + 1][1],
            load=functools.partial(ready, load),
        )
        turn = turn + 2
        found = (found * masks[level - 1]).astype(jnp.bfloat16)
        ordered[:, starts_at[level - 1] : starts_at[level - 1] + pieces[level - 1]] = found
    update = leaf_y.astype(jnp.float32) - gather_product(
        place, 2, found, gathers[8][0], up_1, gathers[8][1]
    )
    ordered[:, :leaf_piece] = gather_product(
        place, 1, update.astype(jnp.bfloat16), leaf_up, upper_leaf, leaf_up_sem,
        load=functools.partial(ready, 13),
    ).astype(jnp.bfloat16)

    parts, core_in, merged, chip_in, trip_sem = back_trip

    def return_step(index, carry):
        at = pl.ds(pl.multiple_of(index * tile, tile), tile)
        moved = jnp.zeros((rhs.shape[0], tile), jnp.float32)
        for inner in range(own_hot.shape[0]):
            moved = moved + times_transposed(
                ordered[:, inner * tile : (inner + 1) * tile], own_hot[inner, at, :]
            )
        moved = moved.astype(jnp.bfloat16)
        parts[2 * index] = moved[:, :LANE]
        parts[2 * index + 1] = moved[:, LANE:]
        return carry

    lax.fori_loop(0, count // 2, return_step, 0)
    exchange(place, parts, core_in, merged, chip_in, wide, trip_sem)

    for index in range(rows_dev // tile):
        moved = jnp.zeros((rhs.shape[0], tile), jnp.float32)
        for inner in range(send_hot.shape[0]):
            moved = moved + times_transposed(
                wide[:, inner * tile : (inner + 1) * tile],
                send_hot[inner, index * tile : (index + 1) * tile, :],
            )
        out[:, index * tile : (index + 1) * tile] = moved.astype(jnp.bfloat16)


def in_one_kernel(
    leaves,
    fronts,
    right_side,
    send_order,
    owner_order,
    live_rows,
    lower_leaf,
    upper_leaf,
    lower_first,
    lower_second,
    lower_third,
    upper_first,
    upper_second,
    upper_third,
    downlink_first,
    downlink_second,
    downlink_third,
    uplink_first,
    uplink_second,
    uplink_third,
    pattern_first,
    pattern_second,
    pattern_third,
):
    columns, rows_dev = right_side.shape
    devices = leaves * fronts
    share = rows_dev // devices
    chips = devices // CORES
    leaf_piece = lower_leaf.shape[1]
    pieces = (lower_first.shape[1], lower_second.shape[1], lower_third.shape[1])
    tile = 2 * LANE
    send_at = jnp.pad(
        send_order.reshape(devices, share), ((0, 0), (0, HALF - share)), constant_values=-1
    ).reshape(-1, 1, tile)
    own_at = (owner_order // share * HALF + owner_order % share).reshape(-1, 1, tile)
    weights = [
        lower_leaf, downlink_first, lower_first, downlink_second, lower_second, downlink_third,
        lower_third, upper_third, uplink_third, upper_second, uplink_second, upper_first,
        uplink_first, upper_leaf,
    ]
    levels = (0, 1, 1, 2, 2, 3, 3, 3, 3, 2, 2, 1, 1, 0)
    weights = [
        weight.reshape(
            2**level * fronts // CORES, CORES, -1, weight.shape[1]
        )
        for weight, level in zip(weights, levels)
    ]
    half = jnp.bfloat16
    dma = pltpu.SemaphoreType.DMA
    scratch = [
        pltpu.VMEM((CORES, weight.shape[0]) + weight.shape[2:], weight.dtype) for weight in weights
    ]
    scratch += [dma((WEIGHTS, CORES))]
    scratch += [
        pltpu.VMEM((chips // 2, rows_dev, tile), half),
        pltpu.VMEM((rows_dev // tile, chips * LANE, tile), half),
        pltpu.VMEM((columns, rows_dev), half),
        pltpu.VMEM((columns, chips * LANE), half),
    ]
    for _ in range(2):
        scratch += [pltpu.VMEM((chips, columns, LANE), half) for _ in range(4)] + [dma((4,))]
    across = fronts // CORES
    for _ in range(2):
        scratch += [pltpu.VMEM((CORES, across, columns, leaf_piece), half), dma((4,))]
    for level in range(1, 4):
        slots = (2**level * across, columns, pieces[level - 1])
        scratch += [pltpu.VMEM((CORES,) + slots, half)]
        scratch += [pltpu.VMEM(slots, half) for _ in range(3)] + [dma((4,))]
    for level in (1, 2, 3, 3, 3, 2, 2, 1, 1):
        slots = (CORES, 2**level * across, columns, pieces[level - 1])
        scratch += [pltpu.VMEM(slots, half), dma((4,))]
    vmem = pl.BlockSpec(memory_space=pltpu.VMEM)
    return pl.pallas_call(
        functools.partial(solve_kernel, leaves, fronts, pieces, leaf_piece),
        out_shape=jax.ShapeDtypeStruct((columns, rows_dev), half),
        in_specs=[vmem, vmem, vmem]
        + [pl.BlockSpec(memory_space=pltpu.SMEM)] * 4
        + [pl.BlockSpec(memory_space=pl.ANY)] * WEIGHTS,
        out_specs=vmem,
        scratch_shapes=scratch,
        compiler_params=pltpu.CompilerParams(
            collective_id=0, has_side_effects=True, vmem_limit_bytes=60 * 2**20
        ),
    )(
        right_side, send_at, own_at, live_rows, pattern_first, pattern_second, pattern_third, *weights
    )


def choose(leaves, fronts, right_side, send_order, owner_order, live_rows, *matrices):
    rows_dev = right_side.shape[1]
    widths = [matrices[index].shape[1] for index in (0, 2, 3, 4)]
    whole_lanes = all(width % LANE == 0 for width in widths)
    whole_lanes = whole_lanes and matrices[6].shape[0] == HALF * matrices[14].shape[0]
    if whole_lanes and rows_dev % (2 * LANE) == 0 and rows_dev // (leaves * fronts) <= HALF:
        run = functools.partial(in_one_kernel, leaves, fronts)
    else:
        run = per_device
    return run(right_side, send_order, owner_order, live_rows, *matrices)


def solution(mesh):
    placed = (
        P(None, ("leaf", "front")),
        P(("leaf", "front")),
        P(("leaf", "front")),
        P(),
        P(None, ("leaf", "front")),
        P(None, ("leaf", "front")),
        P(None, ("leaf", "front")),
        P(None, ("leaf", "front")),
        P(None, ("leaf", "front")),
        P(None, ("leaf", "front")),
        P(None, ("leaf", "front")),
        P(None, ("leaf", "front")),
        P(None, ("leaf", "front")),
        P(None, ("leaf", "front")),
        P(None, ("leaf", "front")),
        P(None, ("leaf", "front")),
        P(None, ("leaf", "front")),
        P(None, ("leaf", "front")),
        P(None, ("leaf", "front")),
        P(None, ("leaf", "front")),
        P(None, ("leaf", "front")),
    )
    return jax.shard_map(
        functools.partial(choose, mesh.shape["leaf"], mesh.shape["front"]),
        mesh=mesh,
        in_specs=placed,
        out_specs=P(None, ("leaf", "front")),
        check_vma=False,
    )
```

```python
import functools

import jax
import jax.numpy as jnp
from jax import lax
from jax.experimental import pallas as pl
from jax.experimental.pallas import tpu as pltpu
from jax.sharding import PartitionSpec as P


def partner_2(value, axis, distance):
    mask = 2**distance
    pairs = [(source, source ^ mask) for source in range(lax.axis_size(axis))]
    return lax.ppermute(value, axis, pairs)


def spread(pattern, block):
    wide = jnp.repeat(pattern, block, axis=0)
    return jnp.repeat(wide, block, axis=1).astype(jnp.bfloat16)


def collect_group(portion, level, place):
    gathered = lax.all_gather(portion, "front", axis=1, tiled=True)
    for level_bit in range(level):
        partner = partner_2(gathered, "leaf", level_bit)
        upper_side = place >> level_bit & 1 == 1
        gathered = jnp.where(
            upper_side,
            jnp.concatenate([partner, gathered], axis=1),
            jnp.concatenate([gathered, partner], axis=1),
        )
    return gathered


def leaf_term(portion, matrix):
    return jnp.dot(portion, matrix, preferred_element_type=jnp.float32)


def per_device(
    right_side,
    send_order,
    owner_order,
    live_rows,
    lower_leaf,
    upper_leaf,
    lower_first,
    lower_second,
    lower_third,
    upper_first,
    upper_second,
    upper_third,
    downlink_first,
    downlink_second,
    downlink_third,
    uplink_first,
    uplink_second,
    uplink_third,
    pattern_first,
    pattern_second,
    pattern_third,
):
    fronts = lax.axis_size("front")
    leaves = lax.axis_size("leaf")
    place = lax.axis_index("leaf")
    column = lax.axis_index("front")
    columns = right_side.shape[0]
    leaf_rows = lower_leaf.shape[1]
    sep = lower_first.shape[0]
    lowers = [lower_first, lower_second, lower_third]
    uppers = [upper_first, upper_second, upper_third]
    downs = [downlink_first, downlink_second, downlink_third]
    backs = [uplink_first, uplink_second, uplink_third]
    patterns = [pattern_first, pattern_second, pattern_third]
    block = downlink_first.shape[0] // pattern_first.shape[0]
    pieces = [lower_first.shape[1], lower_second.shape[1], lower_third.shape[1]]
    starts = [0, leaves // 2, leaves // 2 + leaves // 4]
    outgoing = jnp.take(right_side, send_order, axis=1)
    arrived = lax.all_to_all(outgoing, ("leaf", "front"), split_axis=1, concat_axis=1, tiled=True)
    ordered = jnp.take(arrived, owner_order, axis=1)
    leaf_rhs = ordered[:, :leaf_rows]
    level_rhs = []
    offset = leaf_rows
    for level in range(1, 4):
        level_rhs.append(ordered[:, offset : offset + pieces[level - 1]])
        offset = offset + pieces[level - 1]
    piece_masks = []
    full_masks = []
    within = []
    for level in range(1, 4):
        group = 2**level
        member = place & group - 1
        node_live = lax.dynamic_index_in_dim(
            live_rows, starts[level - 1] + (place >> level), 0, keepdims=False
        )
        first_row = (member * fronts + column) * pieces[level - 1]
        piece_masks.append(
            (first_row + jnp.arange(pieces[level - 1], dtype=jnp.int32) < node_live).astype(
                jnp.float32
            )[None, :]
        )
        full_masks.append(
            (jnp.arange(sep, dtype=jnp.int32) < node_live).astype(jnp.float32)[None, :]
        )
        within.append(member)
    expanded = [spread(patterns[index], block) for index in range(3)]
    leaf_y = leaf_term(
        lax.all_gather(leaf_rhs, "front", axis=1, tiled=True), matrix=lower_leaf
    ).astype(jnp.bfloat16)
    children = leaf_y
    level_y = []
    for level in range(1, 4):
        group = 2**level
        piece = pieces[level - 1]
        member = within[level - 1]
        link = downs[level - 1] * expanded[level - 1]
        own_rhs = level_rhs[level - 1].astype(jnp.float32)
        shaped = link.reshape(group, fronts, piece, link.shape[1])
        term = jnp.einsum(
            "kc,jfpc->kfjp", children, shaped, preferred_element_type=jnp.float32
        ).reshape(columns, sep)
        first_row = (column * group + member) * piece
        current = lax.dynamic_slice_in_dim(term, first_row, piece, 1)
        term = lax.dynamic_update_slice_in_dim(term, current - own_rhs, first_row, 1)
        share = lax.psum_scatter(
            term.astype(jnp.bfloat16), "front", scatter_dimension=1, tiled=True
        ).astype(jnp.float32)
        for level_bit in reversed(range(level)):
            middle = share.shape[1] // 2
            lower_half = share[:, :middle]
            upper_half = share[:, middle:]
            high_side = place >> level_bit & 1 == 1
            keeping = jnp.where(high_side, upper_half, lower_half)
            sending = jnp.where(high_side, lower_half, upper_half)
            share = keeping + partner_2(sending.astype(jnp.bfloat16), "leaf", level_bit).astype(
                sending.dtype
            )
        reduced_piece = (-share * piece_masks[level - 1]).astype(jnp.bfloat16)
        reduced_full = collect_group(reduced_piece, level, place)
        solved = jnp.dot(reduced_full, lowers[level - 1], preferred_element_type=jnp.float32)
        found = (solved * piece_masks[level - 1]).astype(jnp.bfloat16)
        level_y.append(found)
        children = found
    level_x = [None, None, None]
    top_full = collect_group(level_y[2], 3, place)
    level_x[2] = (
        jnp.dot(top_full, upper_third, preferred_element_type=jnp.float32) * piece_masks[2]
    ).astype(jnp.bfloat16)
    for level in (2, 1):
        back = backs[level] * expanded[level]
        parent_full = collect_group(level_x[level], level + 1, place)
        update = level_y[level - 1].astype(jnp.float32) - jnp.dot(
            parent_full, back, preferred_element_type=jnp.float32
        )
        reduced = (update * piece_masks[level - 1]).astype(jnp.bfloat16)
        reduced_full = collect_group(reduced, level, place)
        solved = jnp.dot(reduced_full, uppers[level - 1], preferred_element_type=jnp.float32)
        level_x[level - 1] = (solved * piece_masks[level - 1]).astype(jnp.bfloat16)
    back = uplink_first * expanded[0]
    parent_full = collect_group(level_x[0], 1, place)
    update = (
        leaf_y.astype(jnp.float32) - jnp.dot(parent_full, back, preferred_element_type=jnp.float32)
    ).astype(jnp.bfloat16)
    leaf_x = leaf_term(
        lax.all_gather(update, "front", axis=1, tiled=True), matrix=upper_leaf
    ).astype(jnp.bfloat16)
    placed = jnp.concatenate([leaf_x, level_x[0], level_x[1], level_x[2]], axis=1)
    outbound = jnp.zeros_like(placed).at[:, owner_order].set(placed)
    returned = lax.all_to_all(outbound, ("leaf", "front"), split_axis=1, concat_axis=1, tiled=True)
    return jnp.zeros_like(returned).at[:, send_order].set(returned)


MESH = pl.DeviceIdType.MESH
LANE = 128
HALF = 64
CORES = 2
WEIGHTS = 14


class Place:
    def __init__(self, leaves, fronts):
        self.leaves = leaves
        self.fronts = fronts
        self.across = fronts // CORES
        self.leaf = lax.axis_index("leaf")
        front = lax.axis_index("front")
        self.front = front
        self.x = lax.div(front, CORES)
        self.core = lax.rem(front, CORES)

    def chips(self, group):
        return group * self.across

    def me(self, group):
        return lax.rem(self.leaf, group) * self.across + self.x

    def device(self, group, chip):
        base = self.leaf - lax.rem(self.leaf, group)
        inner = lax.div(chip, self.across)
        return (base + inner, (chip - inner * self.across) * CORES + self.core)

    def sibling(self):
        return (self.leaf, self.x * CORES + 1 - self.core)


def drain(view, sem):
    pltpu.make_async_copy(view, view, sem).wait()


def chip_phase(place, group, source, slots, send_sem, recv_sem):
    count = place.chips(group)
    me = place.me(group)

    def step(r, carry):
        target = lax.rem(me + count - r, count)
        pltpu.make_async_remote_copy(
            src_ref=source(target),
            dst_ref=slots.at[r],
            send_sem=send_sem,
            recv_sem=recv_sem,
            device_id=place.device(group, target),
            device_id_type=MESH,
        ).start()
        return carry

    lax.fori_loop(1, count, step, 0)


def chip_wait(count, slots, sem):
    drain(slots.at[pl.ds(1, count - 1)], sem)


def core_copy(place, source, target, send_sem, recv_sem):
    copy = pltpu.make_async_remote_copy(
        src_ref=source,
        dst_ref=target,
        send_sem=send_sem,
        recv_sem=recv_sem,
        device_id=place.sibling(),
        device_id_type=MESH,
    )
    copy.start()
    return copy


def half_product(slots, weight, core, me):
    count = slots.shape[1]
    pieces = [slots[core, lax.rem(chip + count - me, count)] for chip in range(count)]
    rows = weight[core]
    return jnp.dot(
        jnp.concatenate(pieces, axis=1),
        rows.reshape(count * rows.shape[1], rows.shape[2]),
        preferred_element_type=jnp.float32,
    )


def gather_product(place, group, value, slots, weight, sems, beside=None, load=None):
    count = place.chips(group)
    me = place.me(group)
    mine = slots.at[place.core]
    mine[0] = value
    chip_phase(place, group, lambda target: mine.at[0], mine, sems.at[0], sems.at[1])
    if beside is not None:
        beside()
    chip_wait(count, mine, sems.at[1])
    copy = core_copy(place, mine, mine, sems.at[2], sems.at[3])
    if load is not None:
        load()
    total = half_product(slots, weight, place.core, me)
    copy.wait_recv()
    total = total + half_product(slots, weight, 1 - place.core, me)
    chip_wait(count, mine, sems.at[0])
    copy.wait_send()
    return total


def times_transposed(value, matrix):
    return lax.dot_general(
        value, matrix, (((1,), (1,)), ((), ())), preferred_element_type=jnp.float32
    )


def scatter_sum(place, group, value, link, terms, core_in, summed, chip_in, sems, beside=None):
    count = place.chips(group)
    me = place.me(group)
    width = terms.shape[3]
    each = 512 // width

    def half(core):
        for first in range(0, count, each):
            rows = link[core, first : first + each]
            part = times_transposed(value, rows.reshape(each * width, rows.shape[2]))
            part = part.astype(jnp.bfloat16)
            for inner in range(each):
                terms[core, first + inner] = part[:, inner * width : (inner + 1) * width]

    half(1 - place.core)
    copy = core_copy(place, terms.at[1 - place.core], core_in, sems.at[0], sems.at[1])
    half(place.core)
    copy.wait()
    summed[...] = (
        terms[place.core].astype(jnp.float32) + core_in[...].astype(jnp.float32)
    ).astype(jnp.bfloat16)
    chip_phase(
        place, group, lambda target: summed.at[target], chip_in, sems.at[2], sems.at[3]
    )
    if beside is not None:
        beside()
    chip_wait(count, chip_in, sems.at[3])
    chip_wait(count, chip_in, sems.at[2])
    total = summed[me].astype(jnp.float32)
    for slot in range(1, count):
        total = total + chip_in[slot].astype(jnp.float32)
    return total


def exchange(place, parts, core_in, merged, chip_in, full, sems, first=None, second=None):
    group = place.leaves
    count = place.chips(group)
    me = place.me(group)
    copy = core_copy(place, parts, core_in, sems.at[0], sems.at[1])
    if first is not None:
        first()
    copy.wait()
    lanes = lax.broadcasted_iota(jnp.int32, (parts.shape[1], LANE), 1) // HALF
    own = lanes == place.core

    def merge(chip, carry):
        other = pltpu.roll(core_in[chip].astype(jnp.float32), HALF, 1)
        merged[chip] = jnp.where(own, parts[chip].astype(jnp.float32), other).astype(jnp.bfloat16)
        return carry

    lax.fori_loop(0, count, merge, 0)
    chip_phase(
        place, group, lambda target: merged.at[target], chip_in, sems.at[2], sems.at[3]
    )
    chip_in[0] = merged[me]
    if second is not None:
        second()
    chip_wait(count, chip_in, sems.at[3])
    chip_wait(count, chip_in, sems.at[2])
    for chip in range(count):
        full[:, chip * LANE : (chip + 1) * LANE] = chip_in[lax.rem(chip + count - me, count)]


def fill_hot(target, index):
    rows = 128

    def step(block, carry):
        first = pl.multiple_of(block * rows, rows)
        spots = lax.broadcasted_iota(jnp.int32, (rows, index.shape[1]), 0) + first
        target[pl.ds(first, rows), :] = jnp.where(spots == index, 1.0, 0.0).astype(jnp.bfloat16)
        return carry

    lax.fori_loop(0, target.shape[0] // rows, step, 0)


def solve_kernel(leaves, fronts, pieces, leaf_piece, *refs):
    rhs, send_at, own_at, live = refs[:4]
    patterns = refs[4:7]
    sources = refs[7 : 7 + WEIGHTS]
    out = refs[7 + WEIGHTS]
    scratch = list(refs[8 + WEIGHTS :])

    def take(number):
        taken = scratch[:number]
        del scratch[:number]
        return taken

    weights = take(WEIGHTS)
    (weight_sem,) = take(1)
    send_hot, own_hot = take(2)
    ordered, wide = take(2)
    out_trip = take(5)
    back_trip = take(5)
    leaf_down, leaf_down_sem, leaf_up, leaf_up_sem = take(4)
    sums = [take(5) for _ in range(3)]
    gathers = [take(2) for _ in range(9)]

    place = Place(leaves, fronts)
    count = place.chips(leaves)
    me = place.me(leaves)
    barrier = pltpu.get_barrier_semaphore()

    def greet(r, carry):
        target = lax.rem(me + count - r, count)
        pl.semaphore_signal(
            barrier, inc=1, device_id=place.device(leaves, target), device_id_type=MESH
        )
        return carry

    lax.fori_loop(1, count, greet, 0)
    pl.semaphore_signal(barrier, inc=1, device_id=place.sibling(), device_id_type=MESH)
    loads = [
        [
            pltpu.make_async_copy(
                sources[i].at[:, core], weights[i].at[core], weight_sem.at[i, core]
            )
            for core in range(CORES)
        ]
        for i in range(WEIGHTS)
    ]
    for load in loads:
        for copy in load:
            copy.start()

    def ready(index):
        for copy in loads[index]:
            copy.wait()

    (lower_leaf, down_1, lower_1, down_2, lower_2, down_3, lower_3) = weights[:7]
    (upper_3, up_3, upper_2, up_2, upper_1, up_1, upper_leaf) = weights[7:]

    def masked(index, pattern, part=0, parts=1):
        def run():
            if part == 0:
                ready(index)
            link = weights[index]
            width, columns = link.shape[2:]
            rows = pattern.shape[1]
            block = link.shape[1] * CORES * width // rows
            each = width // block
            low = lax.broadcasted_iota(jnp.int32, (1, LANE), 1) < block

            def step(row, carry):
                kept = [
                    jnp.where(
                        low,
                        pattern[2 * pair, row].astype(jnp.float32),
                        pattern[2 * pair + 1, row].astype(jnp.float32),
                    )
                    for pair in range(columns // LANE)
                ]
                kept = jnp.concatenate(kept, axis=1).astype(jnp.bfloat16)
                piece = lax.div(row, each)
                at = pl.ds(pl.multiple_of((row - piece * each) * block, block), block)
                spot = (lax.rem(piece, CORES), lax.div(piece, CORES), at)
                link[spot] = link[spot] * kept
                return carry

            lax.fori_loop(rows * part // parts, rows * (part + 1) // parts, step, 0)

        return run

    starts = [0, leaves // 2, leaves // 2 + leaves // 4]
    masks = []
    for level in range(1, 4):
        group = 2**level
        piece = pieces[level - 1]
        rows_live = live[starts[level - 1] + place.leaf // group]
        first_row = ((place.leaf % group) * fronts + place.front) * piece
        spots = lax.broadcasted_iota(jnp.int32, (1, piece), 1) + first_row
        masks.append(jnp.where(spots < rows_live, 1.0, 0.0))

    tile = 2 * LANE
    parts, core_in, merged, chip_in, trip_sem = out_trip
    rows_dev = rhs.shape[1]

    def send_step(index, carry):
        fill_hot(send_hot.at[index], send_at[index])
        moved = jnp.dot(rhs[...], send_hot[index], preferred_element_type=jnp.float32)
        moved = moved.astype(jnp.bfloat16)
        parts[2 * index] = moved[:, :LANE]
        parts[2 * index + 1] = moved[:, LANE:]
        return carry

    lax.fori_loop(0, send_hot.shape[0], send_step, 0)
    pl.semaphore_wait(barrier, count)

    def owner_fill():
        def step(index, carry):
            fill_hot(own_hot.at[index], own_at[index])
            return carry

        lax.fori_loop(0, own_hot.shape[0], step, 0)

    exchange(
        place, parts, core_in, merged, chip_in, wide, trip_sem,
        first=owner_fill, second=masked(1, patterns[0]),
    )
    for index in range(own_hot.shape[0]):
        ordered[:, index * tile : (index + 1) * tile] = jnp.dot(
            wide[...], own_hot[index], preferred_element_type=jnp.float32
        ).astype(jnp.bfloat16)

    leaf_y = gather_product(
        place, 1, ordered[:, :leaf_piece], leaf_down, lower_leaf, leaf_down_sem,
        beside=masked(3, patterns[1], 0, 2), load=lambda: ready(0),
    ).astype(jnp.bfloat16)

    child = leaf_y
    level_y = []
    offset = leaf_piece
    chores = [
        masked(3, patterns[1], 1, 2), masked(5, patterns[2], 1, 2), masked(10, patterns[1], 0, 2)
    ]
    late = [masked(5, patterns[2], 0, 2), masked(8, patterns[2]), masked(10, patterns[1], 1, 2)]
    for level in range(1, 4):
        piece = pieces[level - 1]
        total = scatter_sum(
            place, 2**level, child, weights[2 * level - 1], *sums[level - 1],
            beside=chores[level - 1],
        )
        own = ordered[:, offset : offset + piece].astype(jnp.float32)
        offset = offset + piece
        reduced = ((own - total) * masks[level - 1]).astype(jnp.bfloat16)
        solved = gather_product(
            place, 2**level, reduced, gathers[level - 1][0], weights[2 * level],
            gathers[level - 1][1], beside=late[level - 1],
            load=functools.partial(ready, 2 * level),
        )
        child = (solved * masks[level - 1]).astype(jnp.bfloat16)
        level_y.append(child)

    found = gather_product(
        place, 8, level_y[2], gathers[3][0], upper_3, gathers[3][1],
        beside=masked(12, patterns[0], 0, 2), load=functools.partial(ready, 7),
    )
    found = (found * masks[2]).astype(jnp.bfloat16)
    starts_at = [leaf_piece, leaf_piece + pieces[0], leaf_piece + pieces[0] + pieces[1]]
    ordered[:, starts_at[2] : starts_at[2] + pieces[2]] = found
    turn = 4
    for level, back, upper, load in ((2, up_3, upper_2, 9), (1, up_2, upper_1, 11)):
        update = level_y[level - 1].astype(jnp.float32) - gather_product(
            place, 2 ** (level + 1), found, gathers[turn][0], back, gathers[turn][1],
            beside=masked(12, patterns[0], 1, 2) if level == 2 else None,
        )
        reduced = (update * masks[level - 1]).astype(jnp.bfloat16)
        found = gather_product(
            place, 2**level, reduced, gathers[turn + 1][0], upper, gathers[turn + 1][1],
            load=functools.partial(ready, load),
        )
        turn = turn + 2
        found = (found * masks[level - 1]).astype(jnp.bfloat16)
        ordered[:, starts_at[level - 1] : starts_at[level - 1] + pieces[level - 1]] = found
    update = leaf_y.astype(jnp.float32) - gather_product(
        place, 2, found, gathers[8][0], up_1, gathers[8][1]
    )
    ordered[:, :leaf_piece] = gather_product(
        place, 1, update.astype(jnp.bfloat16), leaf_up, upper_leaf, leaf_up_sem,
        load=functools.partial(ready, 13),
    ).astype(jnp.bfloat16)

    parts, core_in, merged, chip_in, trip_sem = back_trip

    def return_step(index, carry):
        at = pl.ds(pl.multiple_of(index * tile, tile), tile)
        moved = jnp.zeros((rhs.shape[0], tile), jnp.float32)
        for inner in range(own_hot.shape[0]):
            moved = moved + times_transposed(
                ordered[:, inner * tile : (inner + 1) * tile], own_hot[inner, at, :]
            )
        moved = moved.astype(jnp.bfloat16)
        parts[2 * index] = moved[:, :LANE]
        parts[2 * index + 1] = moved[:, LANE:]
        return carry

    lax.fori_loop(0, count // 2, return_step, 0)
    exchange(place, parts, core_in, merged, chip_in, wide, trip_sem)

    for index in range(rows_dev // tile):
        moved = jnp.zeros((rhs.shape[0], tile), jnp.float32)
        for inner in range(send_hot.shape[0]):
            moved = moved + times_transposed(
                wide[:, inner * tile : (inner + 1) * tile],
                send_hot[inner, index * tile : (index + 1) * tile, :],
            )
        out[:, index * tile : (index + 1) * tile] = moved.astype(jnp.bfloat16)


def in_one_kernel(
    leaves,
    fronts,
    right_side,
    send_order,
    owner_order,
    live_rows,
    lower_leaf,
    upper_leaf,
    lower_first,
    lower_second,
    lower_third,
    upper_first,
    upper_second,
    upper_third,
    downlink_first,
    downlink_second,
    downlink_third,
    uplink_first,
    uplink_second,
    uplink_third,
    pattern_first,
    pattern_second,
    pattern_third,
):
    columns, rows_dev = right_side.shape
    devices = leaves * fronts
    share = rows_dev // devices
    chips = devices // CORES
    leaf_piece = lower_leaf.shape[1]
    pieces = (lower_first.shape[1], lower_second.shape[1], lower_third.shape[1])
    tile = 2 * LANE
    send_at = jnp.pad(
        send_order.reshape(devices, share), ((0, 0), (0, HALF - share)), constant_values=-1
    ).reshape(-1, 1, tile)
    own_at = (owner_order // share * HALF + owner_order % share).reshape(-1, 1, tile)
    weights = [
        lower_leaf, downlink_first, lower_first, downlink_second, lower_second, downlink_third,
        lower_third, upper_third, uplink_third, upper_second, uplink_second, upper_first,
        uplink_first, upper_leaf,
    ]
    levels = (0, 1, 1, 2, 2, 3, 3, 3, 3, 2, 2, 1, 1, 0)
    weights = [
        weight.reshape(
            2**level * fronts // CORES, CORES, -1, weight.shape[1]
        )
        for weight, level in zip(weights, levels)
    ]
    half = jnp.bfloat16
    dma = pltpu.SemaphoreType.DMA
    scratch = [
        pltpu.VMEM((CORES, weight.shape[0]) + weight.shape[2:], weight.dtype) for weight in weights
    ]
    scratch += [dma((WEIGHTS, CORES))]
    scratch += [
        pltpu.VMEM((chips // 2, rows_dev, tile), half),
        pltpu.VMEM((rows_dev // tile, chips * LANE, tile), half),
        pltpu.VMEM((columns, rows_dev), half),
        pltpu.VMEM((columns, chips * LANE), half),
    ]
    for _ in range(2):
        scratch += [pltpu.VMEM((chips, columns, LANE), half) for _ in range(4)] + [dma((4,))]
    across = fronts // CORES
    for _ in range(2):
        scratch += [pltpu.VMEM((CORES, across, columns, leaf_piece), half), dma((4,))]
    for level in range(1, 4):
        slots = (2**level * across, columns, pieces[level - 1])
        scratch += [pltpu.VMEM((CORES,) + slots, half)]
        scratch += [pltpu.VMEM(slots, half) for _ in range(3)] + [dma((4,))]
    for level in (1, 2, 3, 3, 3, 2, 2, 1, 1):
        slots = (CORES, 2**level * across, columns, pieces[level - 1])
        scratch += [pltpu.VMEM(slots, half), dma((4,))]
    vmem = pl.BlockSpec(memory_space=pltpu.VMEM)
    return pl.pallas_call(
        functools.partial(solve_kernel, leaves, fronts, pieces, leaf_piece),
        out_shape=jax.ShapeDtypeStruct((columns, rows_dev), half),
        in_specs=[vmem, vmem, vmem]
        + [pl.BlockSpec(memory_space=pltpu.SMEM)] * 4
        + [pl.BlockSpec(memory_space=pl.ANY)] * WEIGHTS,
        out_specs=vmem,
        scratch_shapes=scratch,
        compiler_params=pltpu.CompilerParams(
            collective_id=0, has_side_effects=True, vmem_limit_bytes=60 * 2**20
        ),
    )(
        right_side, send_at, own_at, live_rows, pattern_first.T, pattern_second.T,
        pattern_third.T, *weights,
    )


def choose(leaves, fronts, right_side, send_order, owner_order, live_rows, *matrices):
    rows_dev = right_side.shape[1]
    widths = [matrices[index].shape[1] for index in (0, 2, 3, 4)]
    whole_lanes = all(width % LANE == 0 for width in widths)
    whole_lanes = whole_lanes and matrices[6].shape[0] == HALF * matrices[14].shape[0]
    if whole_lanes and rows_dev % (2 * LANE) == 0 and rows_dev // (leaves * fronts) <= HALF:
        run = functools.partial(in_one_kernel, leaves, fronts)
    else:
        run = per_device
    return run(right_side, send_order, owner_order, live_rows, *matrices)


def solution(mesh):
    placed = (
        P(None, ("leaf", "front")),
        P(("leaf", "front")),
        P(("leaf", "front")),
        P(),
        P(None, ("leaf", "front")),
        P(None, ("leaf", "front")),
        P(None, ("leaf", "front")),
        P(None, ("leaf", "front")),
        P(None, ("leaf", "front")),
        P(None, ("leaf", "front")),
        P(None, ("leaf", "front")),
        P(None, ("leaf", "front")),
        P(None, ("leaf", "front")),
        P(None, ("leaf", "front")),
        P(None, ("leaf", "front")),
        P(None, ("leaf", "front")),
        P(None, ("leaf", "front")),
        P(None, ("leaf", "front")),
        P(None, ("leaf", "front")),
        P(None, ("leaf", "front")),
        P(None, ("leaf", "front")),
    )
    return jax.shard_map(
        functools.partial(choose, mesh.shape["leaf"], mesh.shape["front"]),
        mesh=mesh,
        in_specs=placed,
        out_specs=P(None, ("leaf", "front")),
        check_vma=False,
    )
```
